32 devices in a mesh: row: 4 (over y, core), col: 8 (over z, x).
Axes of the slice: x: 2, y: 2, z: 4, core: 2. Of those that a mesh axis runs over, the one named last changes fastest.
Arguments:
- tokens: bfloat16 [256, 8192], P('col', 'row'), may hold values from -6 to 6
- out_grad: bfloat16 [256, 8192], P('col', 'row'), may hold values from -0.119628906 to 0.119628906
- w_gate: bfloat16 [8192, 14336], P('row', 'col'), may hold values from -0.09375 to 0.09375
- w_up: bfloat16 [8192, 14336], P('row', 'col'), may hold values from -0.09375 to 0.09375
- w_down: bfloat16 [8192, 14336], P('row', 'col'), may hold values from -0.0625 to 0.0625
- mask_gate: int32 [64, 112], P('row', 'col'), may hold values 0 or 1
- mask_up: int32 [64, 112], P('row', 'col'), may hold values 0 or 1
- mask_down: int32 [64, 112], P('row', 'col'), may hold values 0 or 1
Outputs:
- mixed: bfloat16 [256, 8192], P('col', 'row')
- grad_gate_w: float32 [8192, 14336], P('row', 'col')
- grad_up_w: float32 [8192, 14336], P('row', 'col')
- grad_down_w: float32 [8192, 14336], P('row', 'col')
The draws below stay inside these ranges and needn't reach their ends.
All inputs are finite; a program needn't handle non-finite values. No bound on the sum of `mask_gate` or of `mask_up` or of `mask_down` on one device may be relied on, other than what follows from the above.
Results may differ from the reference program's by a relative error of at most 0.02.
Values may be sent and summed in bfloat16 or wider, within the bound.
No kernel may reach another device: no remote copies, remote signals or barrier semaphores. Data moves between devices by JAX's collectives and lax.ppermute only.
A program may use at most 192 MiB of HBM per device.

```python
import jax
import jax.numpy as jnp
from jax import lax

D = 8192
FF = 14336
BLOCK = 128
TOKENS = 256
N_ROW = 4
N_COL = 8


def plant(result, key, low, largest):
    spot = [jax.random.randint(jax.random.fold_in(key, axis), (), 0, length) for axis, length in enumerate(result.shape)]
    widest = result.shape.index(max(result.shape))
    neighbour = spot[:widest] + [(spot[widest] + 1) % result.shape[widest]] + spot[widest + 1:]
    return result.at[tuple(spot)].set(low).at[tuple(neighbour)].set(largest)


def levels(own_key, extent, pieces, smallest, largest):
    loudness = 1.0
    for position, blocks in pieces:
        steps = jax.random.uniform(jax.random.fold_in(jax.random.fold_in(own_key, 6), position), (blocks,), jnp.float32, smallest / len(pieces), largest / len(pieces))
        loudness = loudness * jnp.repeat(jnp.exp(steps), extent[position] // blocks).reshape((-1,) + (1,) * (len(extent) - 1 - position))
    return loudness


def normal_values(own_key, extent, scale, reach, split=(), kind=jnp.bfloat16):
    array = jax.random.normal(own_key, extent, jnp.float32) * scale
    if len(split) > 0:
        array = levels(own_key, extent, split, -0.22, 0.18) * array
    return jnp.clip(array, min=-reach, max=reach).astype(kind)


def setup_inputs(seed: int = 0) -> dict:
    streams_of = jax.random.split(jax.random.key(seed), 9)
    tokens = normal_values(streams_of[0], (TOKENS, D), 1.0, 6.0, ((0, 8), (1, 4)))
    out_grad = normal_values(streams_of[1], (TOKENS, D), 0.02, 0.119628906, ((0, 8), (1, 4)))
    w_gate = normal_values(streams_of[2], (D, FF), (D // 2) ** -0.5, 0.09375, ((0, 4), (1, 8)))
    w_up = normal_values(streams_of[3], (D, FF), (D // 2) ** -0.5, 0.09375, ((0, 4), (1, 8)))
    w_down = normal_values(streams_of[4], (D, FF), (FF // 2) ** -0.5, 0.0625, ((0, 4), (1, 8)))
    mask_gate = plant((jax.random.randint(streams_of[5], (D // BLOCK, FF // BLOCK), 0, 2) < 1).astype(jnp.int32), jax.random.fold_in(streams_of[5], 1), 0, 1)
    mask_up = plant((jax.random.randint(streams_of[6], (D // BLOCK, FF // BLOCK), 0, 2) < 1).astype(jnp.int32), jax.random.fold_in(streams_of[6], 1), 0, 1)
    mask_down = plant((jax.random.randint(streams_of[7], (D // BLOCK, FF // BLOCK), 0, 2) < 1).astype(jnp.int32), jax.random.fold_in(streams_of[7], 1), 0, 1)
    return {"tokens": tokens, "out_grad": out_grad, "w_gate": w_gate, "w_up": w_up, "w_down": w_down, "mask_gate": mask_gate, "mask_up": mask_up, "mask_down": mask_down}


def expand(block_mask, weight):
    mask_rows, mask_cols = block_mask.shape
    block_rows = weight.shape[0] // mask_rows
    block_cols = weight.shape[1] // mask_cols
    factor = block_mask.astype(weight.dtype)[:, None, :, None]
    shaped = weight.reshape(mask_rows, block_rows, mask_cols, block_cols) * factor
    return shaped.reshape(weight.shape)


def rounded(value):
    return lax.optimization_barrier(value.astype(jnp.bfloat16)).astype(jnp.float32)


def reference(tokens, out_grad, w_gate, w_up, w_down, mask_gate, mask_up, mask_down):
    gate_m = expand(mask_gate, w_gate)
    up_m = expand(mask_up, w_up)
    down_m = expand(mask_down, w_down)
    width = D // N_ROW
    gate = jnp.zeros((TOKENS, FF), jnp.float32)
    up_sum = jnp.zeros((TOKENS, FF), jnp.float32)
    grad_hidden = jnp.zeros((TOKENS, FF), jnp.float32)
    for index in range(N_ROW):
        lower = index * width
        x_part = tokens[:, lower:lower + width]
        dz_part = out_grad[:, lower:lower + width]
        gate = gate + rounded(jnp.dot(x_part, gate_m[lower:lower + width], preferred_element_type=jnp.float32))
        up_sum = up_sum + rounded(jnp.dot(x_part, up_m[lower:lower + width], preferred_element_type=jnp.float32))
        grad_hidden = grad_hidden + rounded(jnp.dot(dz_part, down_m[lower:lower + width], preferred_element_type=jnp.float32))
    hidden = (jax.nn.silu(gate) * up_sum).astype(jnp.bfloat16)
    span = FF // N_COL
    mixed_sum = jnp.zeros((TOKENS, D), jnp.float32)
    for index in range(N_COL):
        lower = index * span
        mixed_sum = mixed_sum + rounded(jnp.dot(hidden[:, lower:lower + span], down_m[:, lower:lower + span].T, preferred_element_type=jnp.float32))
    mixed = mixed_sum.astype(jnp.bfloat16)
    sigmoid_gate = jax.nn.sigmoid(gate)
    grad_up = (grad_hidden * gate * sigmoid_gate).astype(jnp.bfloat16)
    grad_gate = (grad_hidden * up_sum * sigmoid_gate * (1.0 + gate * (1.0 - sigmoid_gate))).astype(jnp.bfloat16)
    grad_gate_w = expand(mask_gate, jnp.dot(tokens.T, grad_gate, preferred_element_type=jnp.float32))
    grad_up_w = expand(mask_up, jnp.dot(tokens.T, grad_up, preferred_element_type=jnp.float32))
    grad_down_w = expand(mask_down, jnp.dot(out_grad.T, hidden, preferred_element_type=jnp.float32))
    return mixed, grad_gate_w, grad_up_w, grad_down_w
```

```python
import functools

import jax
import jax.numpy as jnp
from jax import lax
from jax.experimental import pallas as pl
from jax.experimental.pallas import tpu as pltpu
from jax.sharding import PartitionSpec as P

BF16 = jnp.bfloat16
F32 = jnp.float32


def tile_of(size, block, most):
    tile = block
    while tile * 2 <= most and size % (tile * 2) == 0:
        tile *= 2
    return tile


def masked_rows(weight, mask_ref, block):
    parts = []
    for index in range(mask_ref.shape[0]):
        row = mask_ref[index].astype(weight.dtype)
        parts.append(weight[index * block:(index + 1) * block, :] * row)
    return parts[0] if len(parts) == 1 else jnp.concatenate(parts, axis=0)


def panel_matmul(core, evens, odds, weights, masks, chunks):
    n_w = len(weights)
    depth, width = weights[0].shape
    half = sum(a.shape[0] for a in evens) // chunks
    blocks = masks[0].shape[0]
    block = depth // blocks
    tile = tile_of(width, 128, 256)
    n_e, n_o = len(evens), len(odds)
    n_k = lax.axis_size("col") // 2
    rows = half // n_k

    def kernel(core_ref, *refs):
        e_refs, o_refs = refs[:n_e], refs[n_e:n_e + n_o]
        w_refs = refs[n_e + n_o:n_e + n_o + n_w]
        m_refs = refs[n_e + n_o + n_w:n_e + n_o + 2 * n_w]
        panel_ref, mine_ref, theirs_ref = refs[n_e + n_o + 2 * n_w:]

        @pl.when(pl.program_id(0) == 0)
        def _():
            for group, place in ((e_refs, core_ref[0]), (o_refs, 1 - core_ref[0])):
                k = 0
                for ref in group:
                    for local in range(ref.shape[0] // (chunks * rows)):
                        for c in range(chunks):
                            start = pl.multiple_of(place * half + (c * 2 * half + k * rows), rows)
                            low = (local * chunks + c) * rows
                            panel_ref[pl.ds(start, rows), :] = ref[low:low + rows, :]
                        k += 1

        for index in range(n_w):
            w = masked_rows(w_refs[index][...], m_refs[index], block)
            out = jnp.dot(panel_ref[...], w, preferred_element_type=F32).astype(BF16)
            for c in range(chunks):
                low = c * 2 * half
                mine_ref[index * chunks + c] = out[low:low + half]
                theirs_ref[index * chunks + c] = out[low + half:low + 2 * half]

    whole = lambda a: pl.BlockSpec(a.shape, lambda n, s: (0,) * a.ndim)
    part = jax.ShapeDtypeStruct((n_w * chunks, half, width), BF16)
    part_spec = pl.BlockSpec((n_w * chunks, half, tile), lambda n, s: (0, 0, n))
    panel = jax.ShapeDtypeStruct((chunks * 2 * half, depth), BF16)
    return pl.pallas_call(
        kernel,
        grid_spec=pltpu.PrefetchScalarGridSpec(
            num_scalar_prefetch=1,
            grid=(width // tile,),
            in_specs=[whole(a) for a in (*evens, *odds)]
            + [pl.BlockSpec((depth, tile), lambda n, s: (0, n))] * n_w
            + [pl.BlockSpec((blocks, 1, tile), lambda n, s: (0, 0, n))] * n_w,
            out_specs=[whole(panel), part_spec, part_spec],
        ),
        out_shape=[panel, part, part],
        compiler_params=pltpu.CompilerParams(vmem_limit_bytes=32 * 2**20),
        cost_estimate=pl.CostEstimate(
            flops=2 * panel.shape[0] * depth * width * n_w,
            bytes_accessed=2 * depth * width * n_w,
            transcendentals=0,
        ),
    )(core, *evens, *odds, *weights, *masks)


def output_matmul(core, hid_mine, hid_theirs, weight, mask):
    depth, width = weight.shape
    half = hid_mine.shape[0]
    block = depth // mask.shape[0]
    tile = tile_of(depth, block, 256)

    def kernel(core_ref, mine_ref, theirs_ref, w_ref, m_ref, even_ref, odd_ref, hid):
        @pl.when(pl.program_id(0) == 0)
        def _():
            hid[pl.ds(pl.multiple_of(core_ref[0] * half, half), half), :] = mine_ref[...]
            hid[pl.ds(pl.multiple_of((1 - core_ref[0]) * half, half), half), :] = theirs_ref[...]

        w = masked_rows(w_ref[...], m_ref, block)
        out = lax.dot_general(
            hid[...], w, (((1,), (1,)), ((), ())), preferred_element_type=F32
        ).astype(BF16)
        even_ref[...] = out[:half]
        odd_ref[...] = out[half:]

    out = jax.ShapeDtypeStruct((half, depth), BF16)
    out_spec = pl.BlockSpec((half, tile), lambda n, s: (0, n))
    return pl.pallas_call(
        kernel,
        grid_spec=pltpu.PrefetchScalarGridSpec(
            num_scalar_prefetch=1,
            grid=(depth // tile,),
            in_specs=[
                pl.BlockSpec((half, width), lambda n, s: (0, 0)),
                pl.BlockSpec((half, width), lambda n, s: (0, 0)),
                pl.BlockSpec((tile, width), lambda n, s: (n, 0)),
                pl.BlockSpec((tile // block, 1, width), lambda n, s: (n, 0, 0)),
            ],
            out_specs=[out_spec, out_spec],
            scratch_shapes=[pltpu.VMEM((2 * half, width), BF16)],
        ),
        out_shape=[out, out],
        compiler_params=pltpu.CompilerParams(vmem_limit_bytes=32 * 2**20),
        cost_estimate=pl.CostEstimate(
            flops=4 * half * depth * width, bytes_accessed=2 * depth * width, transcendentals=0
        ),
    )(core, hid_mine, hid_theirs, weight, mask)


def weight_grads(panels, cots, masks):
    depth = panels[0].shape[1]
    width = cots[0][0].shape[1]
    tokens = sum(p.shape[0] for p in panels)
    block = depth // masks[0].shape[0]
    tile = tile_of(depth, block, 256)
    n_p, n_c, n_o = len(panels), len(cots[0]), len(cots)

    def kernel(*refs):
        p_refs = refs[:n_p]
        c_refs = refs[n_p:n_p + n_c * n_o]
        m_refs = refs[n_p + n_c * n_o:n_p + n_c * n_o + n_o]
        out_refs = refs[n_p + n_c * n_o + n_o:n_p + n_c * n_o + 2 * n_o]
        cot = refs[-1]

        @pl.when(pl.program_id(0) == 0)
        def _():
            for o in range(n_o):
                low = 0
                for ref in c_refs[o * n_c:(o + 1) * n_c]:
                    cot[o, low:low + ref.shape[0], :] = ref[...]
                    low += ref.shape[0]

        lhs = [ref[...] for ref in p_refs]
        lhs = lhs[0] if n_p == 1 else jnp.concatenate(lhs, axis=0)
        for o in range(n_o):
            out = lax.dot_general(
                lhs, cot[o], (((0,), (0,)), ((), ())), preferred_element_type=F32
            )
            for index in range(tile // block):
                out_refs[o][index * block:(index + 1) * block, :] = (
                    out[index * block:(index + 1) * block, :] * m_refs[o][index]
                )

    flat = [a for cot in cots for a in cot]
    out = jax.ShapeDtypeStruct((depth, width), F32)
    return pl.pallas_call(
        kernel,
        grid=(depth // tile,),
        in_specs=[pl.BlockSpec((p.shape[0], tile), lambda n: (0, n)) for p in panels]
        + [pl.BlockSpec(a.shape, lambda n: (0, 0)) for a in flat]
        + [pl.BlockSpec((tile // block, 1, width), lambda n: (n, 0, 0))] * n_o,
        out_specs=[pl.BlockSpec((tile, width), lambda n: (n, 0))] * n_o,
        out_shape=[out] * n_o,
        scratch_shapes=[pltpu.VMEM((n_o, tokens, width), BF16)],
        compiler_params=pltpu.CompilerParams(vmem_limit_bytes=40 * 2**20),
        cost_estimate=pl.CostEstimate(
            flops=2 * tokens * depth * width * n_o,
            bytes_accessed=4 * depth * width * n_o,
            transcendentals=0,
        ),
    )(*panels, *flat, *masks)


def swap(value, axis, bits):
    size = lax.axis_size(axis)
    return lax.ppermute(value, axis, [(i, i ^ bits) for i in range(size)])


def gather_panel(own):
    evens = [own] + [swap(own, "col", 2 * k) for k in range(1, lax.axis_size("col") // 2)]
    odds = [swap(block, "col", 1) for block in evens]
    return evens, odds


def row_sum(mine, theirs):
    pair = (mine.astype(F32) + swap(theirs, "row", 1).astype(F32)).astype(BF16)
    total = pair.astype(F32)
    for k in range(1, lax.axis_size("row") // 2):
        total = total + swap(pair, "row", 2 * k).astype(F32)
    return total


def output_sum(even, odd, rows):
    pair = (even.astype(F32) + swap(odd, "col", 1).astype(F32)).astype(BF16)
    total = pair[:rows].astype(F32)
    for k in range(1, lax.axis_size("col") // 2):
        total = total + swap(pair[k * rows:(k + 1) * rows], "col", 2 * k).astype(F32)
    return total.astype(BF16)


def spread(mask, block):
    return jnp.repeat(mask.astype(F32), block, axis=1)[:, None, :]


def after(value, *earlier):
    return lax.optimization_barrier((value, earlier))[0]


CHUNKS = 2


def per_device(tokens, out_grad, w_gate, w_up, w_down, mask_gate, mask_up, mask_down):
    block = w_gate.shape[1] // mask_gate.shape[1]
    m_gate, m_up, m_down = (spread(m, block) for m in (mask_gate, mask_up, mask_down))
    core = (lax.axis_index("row") % 2).astype(jnp.int32).reshape(1)
    rows = tokens.shape[0] // CHUNKS

    blocks = []
    previous = ()
    for c in range(CHUNKS):
        own = tokens[c * rows:(c + 1) * rows]
        if previous:
            own = after(own, *previous)
        evens, odds = gather_panel(own)
        previous = evens
        blocks.append((evens, odds))
    dz_evens, dz_odds = gather_panel(after(out_grad, *previous))

    panels, gates, ups, hids, sums = [], [], [], [], []
    for evens, odds in blocks:
        panel, mine, theirs = panel_matmul(core, evens, odds, [w_gate, w_up], [m_gate, m_up], 1)
        total = row_sum(mine, theirs)
        panels.append(panel)
        gates.append(total[0])
        ups.append(total[1])
    dz_panel, mine, theirs = panel_matmul(core, dz_evens, dz_odds, [w_down], [m_down], CHUNKS)
    grad_hidden = row_sum(mine, theirs)
    for gate, up in zip(gates, ups):
        hid = (jax.nn.silu(gate) * up).astype(BF16)
        other = swap(hid, "row", 1)
        even, odd = output_matmul(core, hid, other, w_down, m_down)
        sums.append(output_sum(even, odd, rows))
        hids += [hid, other]
    mixed = jnp.concatenate(sums, axis=0)
    (grad_down_w,) = weight_grads([dz_panel], [hids], [m_down])

    gate, up = jnp.stack(gates), jnp.stack(ups)
    s = jax.nn.sigmoid(gate)
    cot = jnp.stack(
        [
            (grad_hidden * up * s * (1.0 + gate * (1.0 - s))).astype(BF16),
            (grad_hidden * gate * s).astype(BF16),
        ]
    )
    other = swap(cot, "row", 1)
    cots = [[a[o, c] for c in range(CHUNKS) for a in (cot, other)] for o in range(2)]
    grad_gate_w, grad_up_w = weight_grads(panels, cots, [m_gate, m_up])
    return (mixed, grad_gate_w, grad_up_w, grad_down_w)


def solution(mesh):
    return jax.shard_map(
        per_device,
        mesh=mesh,
        in_specs=(P("col", "row"),) * 2 + (P("row", "col"),) * 6,
        out_specs=(P("col", "row"),) + (P("row", "col"),) * 3,
        check_vma=False,
    )
```

```python
import functools

import jax
import jax.numpy as jnp
from jax import lax
from jax.experimental import pallas as pl
from jax.experimental.pallas import tpu as pltpu
from jax.sharding import PartitionSpec as P

BF16 = jnp.bfloat16
F32 = jnp.float32


SMALL = 20 * 2**20
LARGE = 32 * 2**20
LITTLE = pl.CostEstimate(flops=1, bytes_accessed=1, transcendentals=0)


def tile_of(size, most=896):
    return max(t for t in range(128, most + 1, 128) if size % t == 0)


def whole_vmem():
    return pl.BlockSpec(memory_space=pltpu.VMEM)


def token_spec():
    return pl.BlockSpec(memory_space=pl.ANY)


TOKEN = jax.ShapeDtypeStruct((8,), jnp.int32)


def hbm(array):
    return pltpu.with_memory_space_constraint(array, pltpu.HBM)


def masked(weight, mask_ref, first, block):
    rows = []
    for i in range(weight.shape[0] // block):
        columns = []
        for j in range(weight.shape[1] // block):
            part = weight[i * block:(i + 1) * block, j * block:(j + 1) * block]
            kept = mask_ref[first + i, j].astype(F32)
            if weight.dtype == BF16:
                factor = jnp.full((16, block), kept).astype(BF16)
                part = part.reshape(block // 16, 16, block) * factor[None]
                columns.append(part.reshape(block, block))
            else:
                columns.append(part * kept)
        rows.append(jnp.concatenate(columns, axis=1) if len(columns) > 1 else columns[0])
    return rows[0] if len(rows) == 1 else jnp.concatenate(rows, axis=0)


def panel_matmul(pieces, arrays, weights, masks, chunks, rows, *earlier):
    n_w = len(weights)
    depth, width = weights[0].shape
    half = len(pieces) // 2 * rows
    step = tile_of(depth, 256)
    block = depth // masks[0].shape[0]
    n_a = len(arrays)
    n_c = len(chunks)

    def kernel(*refs):
        core = lax.axis_index("row") % 2
        a_refs, w_refs = refs[:n_a], refs[n_a:n_a + n_w]
        m_refs = refs[n_a + n_w:n_a + 2 * n_w]
        out_panel, mine_ref, theirs_ref, token_ref, panel_ref, own, held, total, kept, sem, own_sem = refs[-11:]
        mask_copies = [
            pltpu.make_async_copy(m_refs[index], kept.at[index], own_sem.at[2 + index])
            for index in range(n_w)
        ]
        for copy in mask_copies:
            copy.start()
        copies = {}
        for part, low in enumerate(range(0, depth, step)):
            for index in range(n_w):
                at = pl.ds(low, step)
                copies[index, low] = pltpu.make_async_copy(
                    w_refs[index].at[at], held.at[index, at], sem.at[index, part]
                )
        fetch = pltpu.make_async_copy(a_refs[0], own, own_sem.at[0])
        fetch.start()
        for copy in copies.values():
            copy.start()
        fetch.wait()
        a_refs = (own, *a_refs[1:])
        for array, low, odd, k in pieces:
            place = 1 - core if odd else core
            for index, c in enumerate(chunks):
                start = pl.multiple_of(place * half + (index * 2 * half + k * rows), rows)
                panel_ref[pl.ds(start, rows), :] = a_refs[array][pl.ds(low + c * rows, rows), :]
        store = pltpu.make_async_copy(panel_ref, out_panel, own_sem.at[1])
        store.start()
        for copy in mask_copies:
            copy.wait()
        for low in range(0, depth, step):
            for index in range(n_w):
                copies[index, low].wait()
                w = masked(held[index, low:low + step, :], kept.at[index], low // block, block)
                part = jnp.dot(panel_ref[:, low:low + step], w, preferred_element_type=F32)
                if low > 0:
                    part = part + total[index]
                if low + step < depth:
                    total[index] = part
                else:
                    out = part.astype(BF16)
                    for c in range(n_c):
                        top = c * 2 * half
                        mine_ref[index * n_c + c] = out[top:top + half]
                        theirs_ref[index * n_c + c] = out[top + half:top + 2 * half]
        store.wait()

    part = jax.ShapeDtypeStruct((n_w * n_c, half, width), BF16)
    panel = jax.ShapeDtypeStruct((n_c * 2 * half, depth), BF16)
    return pl.pallas_call(
        kernel,
        in_specs=[pl.BlockSpec(memory_space=pl.ANY)]
        + [whole_vmem()] * (n_a - 1)
        + [pl.BlockSpec(memory_space=pl.ANY)] * (2 * n_w)
        + [token_spec()] * len(earlier),
        out_specs=[pl.BlockSpec(memory_space=pl.ANY)] + [whole_vmem()] * 2 + [token_spec()],
        out_shape=[pltpu.HBM(panel.shape, BF16), part, part, TOKEN],
        scratch_shapes=[
            pltpu.VMEM(panel.shape, BF16),
            pltpu.VMEM(arrays[0].shape, BF16),
            pltpu.VMEM((n_w, depth, width), BF16),
            pltpu.VMEM((n_w, *panel.shape[:1], width), F32),
            pltpu.SMEM((n_w, *masks[0].shape), jnp.int32),
            pltpu.SemaphoreType.DMA((n_w, depth // step)),
            pltpu.SemaphoreType.DMA((2 + n_w,)),
        ],
        compiler_params=pltpu.CompilerParams(vmem_limit_bytes=LARGE),
        cost_estimate=LITTLE,
    )(*arrays, *[hbm(w) for w in (*weights, *masks)], *earlier)


def output_matmul(hid_mine, hid_theirs, weight, mask):
    depth, width = weight.shape
    half = hid_mine.shape[0]
    step = tile_of(depth, 512)
    block = depth // mask.shape[0]

    def kernel(mine_ref, theirs_ref, w_ref, m_ref, even_ref, odd_ref, token_ref, hid, held, kept, sem):
        core = lax.axis_index("row") % 2
        mask_copy = pltpu.make_async_copy(m_ref, kept, sem.at[depth // step])
        mask_copy.start()
        copies = {}
        for part, low in enumerate(range(0, depth, step)):
            at = pl.ds(low, step)
            copies[low] = pltpu.make_async_copy(w_ref.at[at], held.at[at], sem.at[part])
        for copy in copies.values():
            copy.start()
        hid[pl.ds(pl.multiple_of(core * half, half), half), :] = mine_ref[...]
        hid[pl.ds(pl.multiple_of((1 - core) * half, half), half), :] = theirs_ref[...]
        mask_copy.wait()
        for low in range(0, depth, step):
            copies[low].wait()
            held[low:low + step, :] = masked(held[low:low + step, :], kept, low // block, block)
            out = lax.dot_general(
                hid[...],
                held[low:low + step, :],
                (((1,), (1,)), ((), ())),
                preferred_element_type=F32,
            ).astype(BF16)
            even_ref[:, low:low + step] = out[:half]
            odd_ref[:, low:low + step] = out[half:]

    out = jax.ShapeDtypeStruct((half, depth), BF16)
    return pl.pallas_call(
        kernel,
        in_specs=[whole_vmem()] * 2 + [pl.BlockSpec(memory_space=pl.ANY)] * 2,
        out_specs=[whole_vmem()] * 2 + [token_spec()],
        out_shape=[out, out, TOKEN],
        scratch_shapes=[
            pltpu.VMEM((2 * half, width), BF16),
            pltpu.VMEM((depth, width), BF16),
            pltpu.SMEM(mask.shape, jnp.int32),
            pltpu.SemaphoreType.DMA((depth // step + 1,)),
        ],
        compiler_params=pltpu.CompilerParams(vmem_limit_bytes=LARGE),
        cost_estimate=LITTLE,
    )(hid_mine, hid_theirs, hbm(weight), hbm(mask))


def join(values, *earlier):
    rows, depth = values[0].shape
    n = len(values)

    def kernel(*refs):
        for index in range(n):
            refs[-2][index * rows:(index + 1) * rows, :] = refs[index][...]

    return pl.pallas_call(
        kernel,
        in_specs=[whole_vmem()] * n + [token_spec()] * len(earlier),
        out_specs=[whole_vmem(), token_spec()],
        out_shape=[jax.ShapeDtypeStruct((n * rows, depth), values[0].dtype), TOKEN],
        compiler_params=pltpu.CompilerParams(vmem_limit_bytes=SMALL),
        cost_estimate=LITTLE,
    )(*values, *earlier)


def add_blocks(first, second, count, *earlier):
    rows = first.shape[0] // count

    def kernel(first_ref, second_ref, *refs):
        for index in range(count):
            at = slice(index * rows, (index + 1) * rows)
            total = first_ref[at].astype(F32) + second_ref[at].astype(F32)
            refs[len(earlier) + index][...] = total.astype(BF16)

    out = jax.ShapeDtypeStruct((rows, *first.shape[1:]), BF16)
    return pl.pallas_call(
        kernel,
        in_specs=[whole_vmem()] * 2 + [token_spec()] * len(earlier),
        out_specs=[whole_vmem()] * count + [token_spec()],
        out_shape=[out] * count + [TOKEN],
        compiler_params=pltpu.CompilerParams(vmem_limit_bytes=SMALL),
        cost_estimate=LITTLE,
    )(first, second, *earlier)


def add_shares(firsts, seconds, count):
    rows = firsts[0].shape[0] // count
    n_c = len(firsts)

    def kernel(*refs):
        for c in range(n_c):
            for index in range(count):
                at = slice(index * rows, (index + 1) * rows)
                total = refs[c][at].astype(F32) + refs[n_c + c][at].astype(F32)
                refs[2 * n_c + index][c * rows:(c + 1) * rows] = total.astype(BF16)

    out = jax.ShapeDtypeStruct((n_c * rows, *firsts[0].shape[1:]), BF16)
    return pl.pallas_call(
        kernel,
        in_specs=[whole_vmem()] * (2 * n_c),
        out_specs=[whole_vmem()] * count + [token_spec()],
        out_shape=[out] * count + [TOKEN],
        compiler_params=pltpu.CompilerParams(vmem_limit_bytes=SMALL),
        cost_estimate=LITTLE,
    )(*firsts, *seconds)


def total_of(refs, at):
    total = refs[0][at].astype(F32)
    for ref in refs[1:]:
        total = total + ref[at].astype(F32)
    return total


def hidden_of(parts, *earlier):
    _, rows, width = parts[0].shape
    n = len(parts)

    def kernel(*refs):
        gate, up = total_of(refs[:n], 0), total_of(refs[:n], 1)
        refs[-2][...] = (jax.nn.silu(gate) * up).astype(BF16)

    return pl.pallas_call(
        kernel,
        in_specs=[whole_vmem()] * n + [token_spec()] * len(earlier),
        out_specs=[whole_vmem(), token_spec()],
        out_shape=[jax.ShapeDtypeStruct((rows, width), BF16), TOKEN],
        compiler_params=pltpu.CompilerParams(vmem_limit_bytes=SMALL),
        cost_estimate=LITTLE,
    )(*parts, *earlier)


def cotangents(chunks, grads, *earlier):
    n_c, rows, width = grads[0].shape
    n, n_g = len(chunks[0]), len(grads)

    def kernel(*refs):
        out_ref = refs[-1]
        for c in range(n_c):
            parts = refs[c * n:(c + 1) * n]
            grad = total_of(refs[n_c * n:n_c * n + n_g], c)
            gate, up = total_of(parts, 0), total_of(parts, 1)
            s = jax.nn.sigmoid(gate)
            out_ref[0, c] = (grad * up * s * (1.0 + gate * (1.0 - s))).astype(BF16)
            out_ref[1, c] = (grad * gate * s).astype(BF16)

    return pl.pallas_call(
        kernel,
        in_specs=[whole_vmem()] * (n_c * n + n_g) + [token_spec()] * len(earlier),
        out_specs=whole_vmem(),
        out_shape=jax.ShapeDtypeStruct((2, n_c, rows, width), BF16),
        compiler_params=pltpu.CompilerParams(vmem_limit_bytes=SMALL),
        cost_estimate=LITTLE,
    )(*[p for c in chunks for p in c], *grads, *earlier)


def weight_grads(panels, cots, masks):
    depth = panels[0].shape[1]
    width = cots[0][0].shape[1]
    tokens = sum(p.shape[0] for p in panels)
    block = depth // masks[0].shape[0]
    tile = tile_of(depth, 256)
    n_p, n_c, n_o = len(panels), len(cots[0]), len(cots)
    slots = 4

    def kernel(*refs):
        p_refs = refs[:n_p]
        c_refs = refs[n_p:n_p + n_c * n_o]
        m_refs = refs[n_p + n_c * n_o:n_p + n_c * n_o + n_o]
        out_refs = refs[-7 - n_o:-7]
        token_ref, cot, panel, out, kept, sem, fetch_sem = refs[-7:]
        low = 0
        fetches = [
            pltpu.make_async_copy(m_refs[o], kept.at[o], fetch_sem.at[n_p + o]) for o in range(n_o)
        ]
        for fetch in fetches:
            fetch.start()
        for index, ref in enumerate(p_refs):
            fetches.append(
                pltpu.make_async_copy(ref, panel.at[pl.ds(low, ref.shape[0])], fetch_sem.at[index])
            )
            fetches[-1].start()
            low += ref.shape[0]
        for o in range(n_o):
            low = 0
            for ref in c_refs[o * n_c:(o + 1) * n_c]:
                cot[o, low:low + ref.shape[0], :] = ref[...]
                low += ref.shape[0]
        for fetch in fetches:
            fetch.wait()
        copies = []
        for low in range(0, depth, tile):
            for o in range(n_o):
                slot = len(copies) % slots
                if len(copies) >= slots:
                    copies[-slots].wait()
                part = lax.dot_general(
                    panel[:, low:low + tile],
                    cot[o],
                    (((0,), (0,)), ((), ())),
                    preferred_element_type=F32,
                )
                out[slot] = masked(part, kept.at[o], low // block, block)
                copies.append(
                    pltpu.make_async_copy(
                        out.at[slot], out_refs[o].at[pl.ds(low, tile)], sem.at[slot]
                    )
                )
                copies[-1].start()
        for copy in copies[-slots:]:
            copy.wait()

    flat = [a for cot in cots for a in cot]
    out = jax.ShapeDtypeStruct((depth, width), F32)
    return pl.pallas_call(
        kernel,
        in_specs=[pl.BlockSpec(memory_space=pl.ANY)] * n_p
        + [whole_vmem()] * len(flat)
        + [pl.BlockSpec(memory_space=pl.ANY)] * n_o,
        out_specs=[pl.BlockSpec(memory_space=pl.ANY)] * n_o + [token_spec()],
        out_shape=[out] * n_o + [TOKEN],
        scratch_shapes=[
            pltpu.VMEM((n_o, tokens, width), BF16),
            pltpu.VMEM((tokens, depth), BF16),
            pltpu.VMEM((slots, tile, width), F32),
            pltpu.SMEM((n_o, *masks[0].shape), jnp.int32),
            pltpu.SemaphoreType.DMA((slots,)),
            pltpu.SemaphoreType.DMA((n_p + n_o,)),
        ],
        compiler_params=pltpu.CompilerParams(vmem_limit_bytes=LARGE),
        cost_estimate=pl.CostEstimate(
            flops=2 * tokens * depth * width * n_o,
            bytes_accessed=4 * depth * width * n_o,
            transcendentals=0,
        ),
    )(*[hbm(p) for p in panels], *flat, *[hbm(m) for m in masks])


def swap(value, axis, bits):
    size = lax.axis_size(axis)
    return lax.ppermute(value, axis, [(i, i ^ bits) for i in range(size)])


def exchange(pair):
    return [pair] + [swap(pair, "row", 2 * k) for k in range(1, lax.axis_size("row") // 2)]


def output_sum(parts, *earlier):
    n = len(parts)

    def kernel(*refs):
        refs[-1][...] = total_of(refs[:n], slice(None)).astype(BF16)

    return pl.pallas_call(
        kernel,
        in_specs=[whole_vmem()] * n + [token_spec()] * len(earlier),
        out_specs=whole_vmem(),
        out_shape=jax.ShapeDtypeStruct(parts[0].shape, BF16),
        compiler_params=pltpu.CompilerParams(vmem_limit_bytes=SMALL),
        cost_estimate=LITTLE,
    )(*parts, *earlier)


CHUNKS = 2


def per_device(tokens, out_grad, w_gate, w_up, w_down, mask_gate, mask_up, mask_down):
    local = tokens.shape[0]
    rows = local // CHUNKS
    n_k = lax.axis_size("col") // 2
    every = range(CHUNKS)

    evens = [tokens] + [swap(tokens, "col", 2 * k) for k in range(1, n_k)]
    x_arrays = [hbm(tokens), *evens[1:]] + [swap(e, "col", 1) for e in evens]
    x_pieces = [(k + odd * n_k, 0, odd, k) for odd in (0, 1) for k in range(n_k)]
    dz_evens = [out_grad] + [swap(out_grad, "col", 2 * k) for k in range(1, n_k)]
    dz_pieces = [(odd, k * local, odd, k) for odd in (0, 1) for k in range(n_k)]

    panels, steps = [], []
    earlier = []
    for c in every:
        panel, mine, theirs, token = panel_matmul(
            x_pieces, x_arrays, [w_gate, w_up], [mask_gate, mask_up], [c], rows, *earlier
        )
        panels.append(panel)
        steps.append((mine, swap(theirs, "row", 1)))
        if c == 0:
            pair, first = add_blocks(*steps[0], 1)
            earlier = [first]
    dz_even, joined = join(dz_evens, token)
    dz_arrays = [dz_even, swap(dz_even, "col", 1)]

    chunks, hids, sums = [], [], []
    parts = exchange(pair)
    for c in every:
        chunks.append(parts)
        hid, formed = hidden_of(parts)
        if c + 1 < CHUNKS:
            pair, added = add_blocks(*steps[c + 1], 1, formed)
            parts = exchange(pair)
        else:
            dz_pair, added = add_blocks(*dz_step, 1, formed)
            grads = exchange(dz_pair)
        other = swap(hid, "row", 1)
        even, odd, token = output_matmul(hid, other, w_down, mask_down)
        sums.append((even, swap(odd, "col", 1)))
        hids += [hid, other]
        if c == 0:
            dz_panel, mine, theirs, token = panel_matmul(
                dz_pieces, dz_arrays, [w_down], [mask_down], every, rows, token
            )
            dz_step = (mine, swap(theirs, "row", 1))
    *shares, summed = add_shares(*zip(*sums), n_k)
    shares = shares[:1] + [swap(shares[k], "col", 2 * k) for k in range(1, n_k)]
    grad_down_w, _ = weight_grads([dz_panel], [hids], [mask_down])

    cot = cotangents(chunks, grads, summed)
    other = swap(cot, "row", 1)
    cots = [[a[o, c] for c in every for a in (cot, other)] for o in range(2)]
    grad_gate_w, grad_up_w, token = weight_grads(panels, cots, [mask_gate, mask_up])
    mixed = output_sum(shares, token)
    return (mixed, grad_gate_w, grad_up_w, grad_down_w)


def solution(mesh):
    return jax.shard_map(
        per_device,
        mesh=mesh,
        in_specs=(P("col", "row"),) * 2 + (P("row", "col"),) * 6,
        out_specs=(P("col", "row"),) + (P("row", "col"),) * 3,
        check_vma=False,
    )
```

```python
import functools

import jax
import jax.numpy as jnp
from jax import lax
from jax.experimental import pallas as pl
from jax.experimental.pallas import tpu as pltpu
from jax.sharding import PartitionSpec as P

BF16 = jnp.bfloat16
F32 = jnp.float32


SMALL = 20 * 2**20
LARGE = 32 * 2**20
LITTLE = pl.CostEstimate(flops=1, bytes_accessed=1, transcendentals=0)


def tile_of(size, most=896):
    return max(t for t in range(128, most + 1, 128) if size % t == 0)


def whole_vmem():
    return pl.BlockSpec(memory_space=pltpu.VMEM)


def token_spec():
    return pl.BlockSpec(memory_space=pl.ANY)


TOKEN = jax.ShapeDtypeStruct((8,), jnp.int32)


def hbm(array):
    return pltpu.with_memory_space_constraint(array, pltpu.HBM)


def masked(weight, mask_ref, first, block):
    rows = []
    for i in range(weight.shape[0] // block):
        columns = []
        for j in range(weight.shape[1] // block):
            part = weight[i * block:(i + 1) * block, j * block:(j + 1) * block]
            kept = mask_ref[first + i, j].astype(F32)
            if weight.dtype == BF16:
                factor = jnp.full((16, block), kept).astype(BF16)
                part = part.reshape(block // 16, 16, block) * factor[None]
                columns.append(part.reshape(block, block))
            else:
                columns.append(part * kept)
        rows.append(jnp.concatenate(columns, axis=1) if len(columns) > 1 else columns[0])
    return rows[0] if len(rows) == 1 else jnp.concatenate(rows, axis=0)


def panel_matmul(pieces, arrays, weights, masks, rows, *earlier):
    n_w = len(weights)
    depth, width = weights[0].shape
    n_c = 1 + max(piece[2] for piece in pieces)
    half = len(pieces) // (2 * n_c) * rows
    step = tile_of(depth, 256)
    block = depth // masks[0].shape[0]
    n_a = len(arrays)

    def kernel(*refs):
        core = lax.axis_index("row") % 2
        a_refs, w_refs = refs[:n_a], refs[n_a:n_a + n_w]
        m_refs = refs[n_a + n_w:n_a + 2 * n_w]
        out_panel, mine_ref, theirs_ref, token_ref, panel_ref, held, total, kept, sem, one_sem = refs[-10:]
        mask_copies = [
            pltpu.make_async_copy(m_refs[index], kept.at[index], one_sem.at[index])
            for index in range(n_w)
        ]
        for copy in mask_copies:
            copy.start()
        copies = {}
        for part, low in enumerate(range(0, depth, step)):
            for index in range(n_w):
                at = pl.ds(low, step)
                copies[index, low] = pltpu.make_async_copy(
                    w_refs[index].at[at], held.at[index, at], sem.at[index, part]
                )
        for copy in copies.values():
            copy.start()
        for array, low, chunk, part, k in pieces:
            place = 1 - core if part else core
            start = pl.multiple_of(place * half + (chunk * 2 * half + k * rows), rows)
            panel_ref[pl.ds(start, rows), :] = a_refs[array][pl.ds(low, rows), :]
        store = pltpu.make_async_copy(panel_ref, out_panel, one_sem.at[n_w])
        store.start()
        for copy in mask_copies:
            copy.wait()
        for low in range(0, depth, step):
            for index in range(n_w):
                copies[index, low].wait()
                w = masked(held[index, low:low + step, :], kept.at[index], low // block, block)
                part = jnp.dot(panel_ref[:, low:low + step], w, preferred_element_type=F32)
                if low > 0:
                    part = part + total[index]
                if low + step < depth:
                    total[index] = part
                else:
                    out = part.astype(BF16)
                    for c in range(n_c):
                        top = c * 2 * half
                        mine_ref[index * n_c + c] = out[top:top + half]
                        theirs_ref[index * n_c + c] = out[top + half:top + 2 * half]
        store.wait()

    part = jax.ShapeDtypeStruct((n_w * n_c, half, width), BF16)
    panel = jax.ShapeDtypeStruct((n_c * 2 * half, depth), BF16)
    return pl.pallas_call(
        kernel,
        in_specs=[whole_vmem()] * n_a
        + [pl.BlockSpec(memory_space=pl.ANY)] * (2 * n_w)
        + [token_spec()] * len(earlier),
        out_specs=[pl.BlockSpec(memory_space=pl.ANY)] + [whole_vmem()] * 2 + [token_spec()],
        out_shape=[pltpu.HBM(panel.shape, BF16), part, part, TOKEN],
        scratch_shapes=[
            pltpu.VMEM(panel.shape, BF16),
            pltpu.VMEM((n_w, depth, width), BF16),
            pltpu.VMEM((n_w, *panel.shape[:1], width), F32),
            pltpu.SMEM((n_w, *masks[0].shape), jnp.int32),
            pltpu.SemaphoreType.DMA((n_w, depth // step)),
            pltpu.SemaphoreType.DMA((1 + n_w,)),
        ],
        compiler_params=pltpu.CompilerParams(vmem_limit_bytes=LARGE),
        cost_estimate=LITTLE,
    )(*arrays, *[hbm(w) for w in (*weights, *masks)], *earlier)


def output_matmul(hid_mine, hid_theirs, weight, mask, count):
    depth, width = weight.shape
    half = hid_mine.shape[0]
    rows = 2 * half // count
    step = tile_of(depth, 512)
    block = depth // mask.shape[0]

    def kernel(mine_ref, theirs_ref, w_ref, m_ref, *refs):
        out_refs = refs[:count]
        token_ref, hid, held, kept, sem = refs[count:]
        core = lax.axis_index("row") % 2
        mask_copy = pltpu.make_async_copy(m_ref, kept, sem.at[depth // step])
        mask_copy.start()
        copies = {}
        for part, low in enumerate(range(0, depth, step)):
            at = pl.ds(low, step)
            copies[low] = pltpu.make_async_copy(w_ref.at[at], held.at[at], sem.at[part])
        for copy in copies.values():
            copy.start()
        hid[pl.ds(pl.multiple_of(core * half, half), half), :] = mine_ref[...]
        hid[pl.ds(pl.multiple_of((1 - core) * half, half), half), :] = theirs_ref[...]
        mask_copy.wait()
        for low in range(0, depth, step):
            copies[low].wait()
            held[low:low + step, :] = masked(held[low:low + step, :], kept, low // block, block)
            out = lax.dot_general(
                hid[...],
                held[low:low + step, :],
                (((1,), (1,)), ((), ())),
                preferred_element_type=F32,
            ).astype(BF16)
            for k in range(count):
                out_refs[k][:, low:low + step] = out[k * rows:(k + 1) * rows]

    out = jax.ShapeDtypeStruct((rows, depth), BF16)
    return pl.pallas_call(
        kernel,
        in_specs=[whole_vmem()] * 2 + [pl.BlockSpec(memory_space=pl.ANY)] * 2,
        out_specs=[whole_vmem()] * count + [token_spec()],
        out_shape=[out] * count + [TOKEN],
        scratch_shapes=[
            pltpu.VMEM((2 * half, width), BF16),
            pltpu.VMEM((depth, width), BF16),
            pltpu.SMEM(mask.shape, jnp.int32),
            pltpu.SemaphoreType.DMA((depth // step + 1,)),
        ],
        compiler_params=pltpu.CompilerParams(vmem_limit_bytes=LARGE),
        cost_estimate=LITTLE,
    )(hid_mine, hid_theirs, hbm(weight), hbm(mask))


def join(values, *earlier):
    rows, depth = values[0].shape
    n = len(values)

    def kernel(*refs):
        for index in range(n):
            refs[-2][index * rows:(index + 1) * rows, :] = refs[index][...]

    return pl.pallas_call(
        kernel,
        in_specs=[whole_vmem()] * n + [token_spec()] * len(earlier),
        out_specs=[whole_vmem(), token_spec()],
        out_shape=[jax.ShapeDtypeStruct((n * rows, depth), values[0].dtype), TOKEN],
        compiler_params=pltpu.CompilerParams(vmem_limit_bytes=SMALL),
        cost_estimate=LITTLE,
    )(*values, *earlier)


def add_blocks(first, second, count, *earlier):
    rows = first.shape[0] // count

    def kernel(first_ref, second_ref, *refs):
        for index in range(count):
            at = slice(index * rows, (index + 1) * rows)
            total = first_ref[at].astype(F32) + second_ref[at].astype(F32)
            refs[len(earlier) + index][...] = total.astype(BF16)

    out = jax.ShapeDtypeStruct((rows, *first.shape[1:]), BF16)
    return pl.pallas_call(
        kernel,
        in_specs=[whole_vmem()] * 2 + [token_spec()] * len(earlier),
        out_specs=[whole_vmem()] * count + [token_spec()],
        out_shape=[out] * count + [TOKEN],
        compiler_params=pltpu.CompilerParams(vmem_limit_bytes=SMALL),
        cost_estimate=LITTLE,
    )(first, second, *earlier)


def total_of(refs, at):
    total = refs[0][at].astype(F32)
    for ref in refs[1:]:
        total = total + ref[at].astype(F32)
    return total


def hidden_of(parts, *earlier):
    _, rows, width = parts[0].shape
    n = len(parts)

    def kernel(*refs):
        gate, up = total_of(refs[:n], 0), total_of(refs[:n], 1)
        refs[-2][...] = (jax.nn.silu(gate) * up).astype(BF16)

    return pl.pallas_call(
        kernel,
        in_specs=[whole_vmem()] * n + [token_spec()] * len(earlier),
        out_specs=[whole_vmem(), token_spec()],
        out_shape=[jax.ShapeDtypeStruct((rows, width), BF16), TOKEN],
        compiler_params=pltpu.CompilerParams(vmem_limit_bytes=SMALL),
        cost_estimate=LITTLE,
    )(*parts, *earlier)


def cotangents(chunks, grads, *earlier):
    n_c, rows, width = grads[0].shape
    n, n_g = len(chunks[0]), len(grads)

    def kernel(*refs):
        out_ref = refs[-1]
        for c in range(n_c):
            parts = refs[c * n:(c + 1) * n]
            grad = total_of(refs[n_c * n:n_c * n + n_g], c)
            gate, up = total_of(parts, 0), total_of(parts, 1)
            s = jax.nn.sigmoid(gate)
            out_ref[0, c] = (grad * up * s * (1.0 + gate * (1.0 - s))).astype(BF16)
            out_ref[1, c] = (grad * gate * s).astype(BF16)

    return pl.pallas_call(
        kernel,
        in_specs=[whole_vmem()] * (n_c * n + n_g) + [token_spec()] * len(earlier),
        out_specs=whole_vmem(),
        out_shape=jax.ShapeDtypeStruct((2, n_c, rows, width), BF16),
        compiler_params=pltpu.CompilerParams(vmem_limit_bytes=max(SMALL, 48 * n_c * rows * width)),
        cost_estimate=LITTLE,
    )(*[p for c in chunks for p in c], *grads, *earlier)


def weight_grads(panels, cots, masks, *earlier, cost=None):
    depth = panels[0].shape[1]
    width = cots[0][0].shape[1]
    tokens = sum(p.shape[0] for p in panels)
    block = depth // masks[0].shape[0]
    tile = tile_of(depth, 256)
    n_p, n_c, n_o = len(panels), len(cots[0]), len(cots)
    slots = 4

    def kernel(*refs):
        p_refs = refs[:n_p]
        c_refs = refs[n_p:n_p + n_c * n_o]
        m_refs = refs[n_p + n_c * n_o:n_p + n_c * n_o + n_o]
        out_refs = refs[-7 - n_o:-7]
        token_ref, cot, panel, out, kept, sem, fetch_sem = refs[-7:]
        low = 0
        fetches = [
            pltpu.make_async_copy(m_refs[o], kept.at[o], fetch_sem.at[n_p + o]) for o in range(n_o)
        ]
        for fetch in fetches:
            fetch.start()
        for index, ref in enumerate(p_refs):
            fetches.append(
                pltpu.make_async_copy(ref, panel.at[pl.ds(low, ref.shape[0])], fetch_sem.at[index])
            )
            fetches[-1].start()
            low += ref.shape[0]
        for o in range(n_o):
            low = 0
            for ref in c_refs[o * n_c:(o + 1) * n_c]:
                cot[o, low:low + ref.shape[0], :] = ref[...]
                low += ref.shape[0]
        for fetch in fetches:
            fetch.wait()
        copies = []
        for low in range(0, depth, tile):
            for o in range(n_o):
                slot = len(copies) % slots
                if len(copies) >= slots:
                    copies[-slots].wait()
                part = lax.dot_general(
                    panel[:, low:low + tile],
                    cot[o],
                    (((0,), (0,)), ((), ())),
                    preferred_element_type=F32,
                )
                out[slot] = masked(part, kept.at[o], low // block, block)
                copies.append(
                    pltpu.make_async_copy(
                        out.at[slot], out_refs[o].at[pl.ds(low, tile)], sem.at[slot]
                    )
                )
                copies[-1].start()
        for copy in copies[-slots:]:
            copy.wait()

    flat = [a for cot in cots for a in cot]
    out = jax.ShapeDtypeStruct((depth, width), F32)
    return pl.pallas_call(
        kernel,
        in_specs=[pl.BlockSpec(memory_space=pl.ANY)] * n_p
        + [whole_vmem()] * len(flat)
        + [pl.BlockSpec(memory_space=pl.ANY)] * n_o
        + [token_spec()] * len(earlier),
        out_specs=[pl.BlockSpec(memory_space=pl.ANY)] * n_o + [token_spec()],
        out_shape=[out] * n_o + [TOKEN],
        scratch_shapes=[
            pltpu.VMEM((n_o, tokens, width), BF16),
            pltpu.VMEM((tokens, depth), BF16),
            pltpu.VMEM((slots, tile, width), F32),
            pltpu.SMEM((n_o, *masks[0].shape), jnp.int32),
            pltpu.SemaphoreType.DMA((slots,)),
            pltpu.SemaphoreType.DMA((n_p + n_o,)),
        ],
        compiler_params=pltpu.CompilerParams(vmem_limit_bytes=LARGE),
        cost_estimate=cost
        or pl.CostEstimate(
            flops=2 * tokens * depth * width * n_o,
            bytes_accessed=4 * depth * width * n_o,
            transcendentals=0,
        ),
    )(*[hbm(p) for p in panels], *flat, *[hbm(m) for m in masks], *earlier)


def swap(value, axis, bits):
    size = lax.axis_size(axis)
    return lax.ppermute(value, axis, [(i, i ^ bits) for i in range(size)])


def exchange(pair):
    return [pair] + [swap(pair, "row", 2 * k) for k in range(1, lax.axis_size("row") // 2)]


def output_sum(parts, dtype, *earlier):
    n = len(parts)

    def kernel(*refs):
        refs[-2][...] = total_of(refs[:n], slice(None)).astype(dtype)

    return pl.pallas_call(
        kernel,
        in_specs=[whole_vmem()] * n + [token_spec()] * len(earlier),
        out_specs=[whole_vmem(), token_spec()],
        out_shape=[jax.ShapeDtypeStruct(parts[0].shape, dtype), TOKEN],
        compiler_params=pltpu.CompilerParams(vmem_limit_bytes=SMALL),
        cost_estimate=LITTLE,
    )(*parts, *earlier)


def per_device(tokens, out_grad, w_gate, w_up, w_down, mask_gate, mask_up, mask_down):
    rows = tokens.shape[0]
    n_k = lax.axis_size("col") // 2
    part = n_k // 2

    def places(chunk, k):
        return chunk, k // part, k % part

    evens = [tokens] + [swap(tokens, "col", 2 * k) for k in range(1, n_k)]
    own, swapped = join([tokens, swap(tokens, "col", 1)])
    panel, mine, theirs, token = panel_matmul(
        [(k, 0, *places(0, k)) for k in range(n_k)],
        [own, *evens[1:]],
        [w_gate, w_up],
        [mask_gate, mask_up],
        rows,
        swapped,
    )
    rest, _ = join(evens[1:], token)
    rest_odd = swap(rest, "col", 1)
    pair, first = add_blocks(mine, swap(theirs, "row", 1), 1)
    parts = exchange(pair)
    dz_even, joined = join([out_grad] + [swap(out_grad, "col", 2 * k) for k in range(1, n_k)], first)
    panel_odd, mine, theirs, token = panel_matmul(
        [(min(k, 1), max(k - 1, 0) * rows if k else rows, *places(0, k)) for k in range(n_k)],
        [own, rest_odd],
        [w_gate, w_up],
        [mask_gate, mask_up],
        rows,
        first,
        joined,
    )
    panels = [panel, panel_odd]
    step = (mine, swap(theirs, "row", 1))

    dz_arrays = [dz_even, swap(dz_even, "col", 1)]
    dz_pieces = [(c, k * rows, *places(c, k)) for c in range(2) for k in range(n_k)]

    chunks, hids, outs = [], [], []
    for c in range(2):
        chunks.append(parts)
        hid, formed = hidden_of(parts)
        pair, added = add_blocks(*step, 1, formed)
        parts = exchange(pair)
        other = swap(hid, "row", 1)
        *out, token = output_matmul(hid, other, w_down, mask_down, n_k)
        outs.append(out)
        hids += [hid, other]
        if c == 0:
            dz_panel, mine, theirs, token = panel_matmul(
                dz_pieces, dz_arrays, [w_down], [mask_down], rows, token
            )
            step = (mine, swap(theirs, "row", 1))
    own_share = outs[0][:1] + [swap(outs[0][k], "col", 2 * k) for k in range(1, n_k)]
    grad_down_w, token = weight_grads([dz_panel], [hids], [mask_down], token, cost=LITTLE)
    own_share, token = output_sum(own_share, F32, token)
    shares = [own_share] + [swap(outs[1][k], "col", 2 * k + 1) for k in range(n_k)]

    cot = cotangents(chunks, parts, token)
    other = swap(cot, "row", 1)
    cots = [[a[o, c] for c in range(2) for a in (cot, other)] for o in range(2)]
    grad_gate_w, grad_up_w, token = weight_grads(panels, cots, [mask_gate, mask_up])
    mixed, _ = output_sum(shares, BF16, token)
    return (mixed, grad_gate_w, grad_up_w, grad_down_w)


def solution(mesh):
    return jax.shard_map(
        per_device,
        mesh=mesh,
        in_specs=(P("col", "row"),) * 2 + (P("row", "col"),) * 6,
        out_specs=(P("col", "row"),) + (P("row", "col"),) * 3,
        check_vma=False,
    )
```

```python
import functools

import jax
import jax.numpy as jnp
from jax import lax
from jax.experimental import pallas as pl
from jax.experimental.pallas import tpu as pltpu
from jax.sharding import PartitionSpec as P

BF16 = jnp.bfloat16
F32 = jnp.float32


SMALL = 20 * 2**20
LARGE = 32 * 2**20
LITTLE = pl.CostEstimate(flops=1, bytes_accessed=1, transcendentals=0)


def tile_of(size, most=896):
    return max(t for t in range(128, most + 1, 128) if size % t == 0)


def whole_vmem():
    return pl.BlockSpec(memory_space=pltpu.VMEM)


def token_spec():
    return pl.BlockSpec(memory_space=pl.ANY)


TOKEN = jax.ShapeDtypeStruct((8,), jnp.int32)


def hbm(array):
    return pltpu.with_memory_space_constraint(array, pltpu.HBM)


def masked(weight, mask_ref, first, block):
    rows = []
    for i in range(weight.shape[0] // block):
        columns = []
        for j in range(weight.shape[1] // block):
            part = weight[i * block:(i + 1) * block, j * block:(j + 1) * block]
            kept = mask_ref[first + i, j].astype(F32)
            if weight.dtype == BF16:
                factor = jnp.full((16, block), kept).astype(BF16)
                part = part.reshape(block // 16, 16, block) * factor[None]
                columns.append(part.reshape(block, block))
            else:
                columns.append(part * kept)
        rows.append(jnp.concatenate(columns, axis=1) if len(columns) > 1 else columns[0])
    return rows[0] if len(rows) == 1 else jnp.concatenate(rows, axis=0)


def panel_matmul(pieces, arrays, weights, masks, rows, *earlier):
    n_w = len(weights)
    depth, width = weights[0].shape
    n_c = 1 + max(piece[2] for piece in pieces)
    half = len(pieces) // (2 * n_c) * rows
    step = tile_of(depth, 256)
    block = depth // masks[0].shape[0]
    n_a = len(arrays)

    def kernel(*refs):
        core = lax.axis_index("row") % 2
        a_refs, w_refs = refs[:n_a], refs[n_a:n_a + n_w]
        m_refs = refs[n_a + n_w:n_a + 2 * n_w]
        out_panel, mine_ref, theirs_ref, token_ref, panel_ref, held, total, kept, sem, one_sem = refs[-10:]
        mask_copies = [
            pltpu.make_async_copy(m_refs[index], kept.at[index], one_sem.at[index])
            for index in range(n_w)
        ]
        for copy in mask_copies:
            copy.start()
        copies = {}
        for part, low in enumerate(range(0, depth, step)):
            for index in range(n_w):
                at = pl.ds(low, step)
                copies[index, low] = pltpu.make_async_copy(
                    w_refs[index].at[at], held.at[index, at], sem.at[index, part]
                )
        for copy in copies.values():
            copy.start()
        for array, low, chunk, part, k in pieces:
            place = 1 - core if part else core
            start = pl.multiple_of(place * half + (chunk * 2 * half + k * rows), rows)
            panel_ref[pl.ds(start, rows), :] = a_refs[array][pl.ds(low, rows), :]
        store = pltpu.make_async_copy(panel_ref, out_panel, one_sem.at[n_w])
        store.start()
        for copy in mask_copies:
            copy.wait()
        for low in range(0, depth, step):
            for index in range(n_w):
                copies[index, low].wait()
                w = masked(held[index, low:low + step, :], kept.at[index], low // block, block)
                part = jnp.dot(panel_ref[:, low:low + step], w, preferred_element_type=F32)
                if low > 0:
                    part = part + total[index]
                if low + step < depth:
                    total[index] = part
                else:
                    out = part.astype(BF16)
                    for c in range(n_c):
                        top = c * 2 * half
                        mine_ref[index * n_c + c] = out[top:top + half]
                        theirs_ref[index * n_c + c] = out[top + half:top + 2 * half]
        store.wait()

    part = jax.ShapeDtypeStruct((n_w * n_c, half, width), BF16)
    panel = jax.ShapeDtypeStruct((n_c * 2 * half, depth), BF16)
    return pl.pallas_call(
        kernel,
        in_specs=[whole_vmem()] * n_a
        + [pl.BlockSpec(memory_space=pl.ANY)] * (2 * n_w)
        + [token_spec()] * len(earlier),
        out_specs=[pl.BlockSpec(memory_space=pl.ANY)] + [whole_vmem()] * 2 + [token_spec()],
        out_shape=[pltpu.HBM(panel.shape, BF16), part, part, TOKEN],
        scratch_shapes=[
            pltpu.VMEM(panel.shape, BF16),
            pltpu.VMEM((n_w, depth, width), BF16),
            pltpu.VMEM((n_w, *panel.shape[:1], width), F32),
            pltpu.SMEM((n_w, *masks[0].shape), jnp.int32),
            pltpu.SemaphoreType.DMA((n_w, depth // step)),
            pltpu.SemaphoreType.DMA((1 + n_w,)),
        ],
        compiler_params=pltpu.CompilerParams(vmem_limit_bytes=LARGE),
        cost_estimate=LITTLE,
    )(*arrays, *[hbm(w) for w in (*weights, *masks)], *earlier)


def output_matmul(hid_mine, hid_theirs, weight, mask, count):
    depth, width = weight.shape
    half = hid_mine.shape[0]
    rows = 2 * half // count
    step = tile_of(depth, 512)
    block = depth // mask.shape[0]

    def kernel(mine_ref, theirs_ref, w_ref, m_ref, *refs):
        out_refs = refs[:count]
        token_ref, hid, held, kept, sem = refs[count:]
        core = lax.axis_index("row") % 2
        mask_copy = pltpu.make_async_copy(m_ref, kept, sem.at[depth // step])
        mask_copy.start()
        copies = {}
        for part, low in enumerate(range(0, depth, step)):
            at = pl.ds(low, step)
            copies[low] = pltpu.make_async_copy(w_ref.at[at], held.at[at], sem.at[part])
        for copy in copies.values():
            copy.start()
        hid[pl.ds(pl.multiple_of(core * half, half), half), :] = mine_ref[...]
        hid[pl.ds(pl.multiple_of((1 - core) * half, half), half), :] = theirs_ref[...]
        mask_copy.wait()
        for low in range(0, depth, step):
            copies[low].wait()
            held[low:low + step, :] = masked(held[low:low + step, :], kept, low // block, block)
            out = lax.dot_general(
                hid[...],
                held[low:low + step, :],
                (((1,), (1,)), ((), ())),
                preferred_element_type=F32,
            ).astype(BF16)
            for k in range(count):
                out_refs[k][:, low:low + step] = out[k * rows:(k + 1) * rows]

    out = jax.ShapeDtypeStruct((rows, depth), BF16)
    return pl.pallas_call(
        kernel,
        in_specs=[whole_vmem()] * 2 + [pl.BlockSpec(memory_space=pl.ANY)] * 2,
        out_specs=[whole_vmem()] * count + [token_spec()],
        out_shape=[out] * count + [TOKEN],
        scratch_shapes=[
            pltpu.VMEM((2 * half, width), BF16),
            pltpu.VMEM((depth, width), BF16),
            pltpu.SMEM(mask.shape, jnp.int32),
            pltpu.SemaphoreType.DMA((depth // step + 1,)),
        ],
        compiler_params=pltpu.CompilerParams(vmem_limit_bytes=LARGE),
        cost_estimate=LITTLE,
    )(hid_mine, hid_theirs, hbm(weight), hbm(mask))


def join(values, *earlier):
    rows, depth = values[0].shape
    n = len(values)

    def kernel(*refs):
        for index in range(n):
            refs[-2][index * rows:(index + 1) * rows, :] = refs[index][...]

    return pl.pallas_call(
        kernel,
        in_specs=[whole_vmem()] * n + [token_spec()] * len(earlier),
        out_specs=[whole_vmem(), token_spec()],
        out_shape=[jax.ShapeDtypeStruct((n * rows, depth), values[0].dtype), TOKEN],
        compiler_params=pltpu.CompilerParams(vmem_limit_bytes=SMALL),
        cost_estimate=LITTLE,
    )(*values, *earlier)


def add_blocks(first, second, count, *earlier):
    rows = first.shape[0] // count

    def kernel(first_ref, second_ref, *refs):
        for index in range(count):
            at = slice(index * rows, (index + 1) * rows)
            total = first_ref[at].astype(F32) + second_ref[at].astype(F32)
            refs[len(earlier) + index][...] = total.astype(BF16)

    out = jax.ShapeDtypeStruct((rows, *first.shape[1:]), BF16)
    return pl.pallas_call(
        kernel,
        in_specs=[whole_vmem()] * 2 + [token_spec()] * len(earlier),
        out_specs=[whole_vmem()] * count + [token_spec()],
        out_shape=[out] * count + [TOKEN],
        compiler_params=pltpu.CompilerParams(vmem_limit_bytes=SMALL),
        cost_estimate=LITTLE,
    )(first, second, *earlier)


def total_of(refs, at):
    total = refs[0][at].astype(F32)
    for ref in refs[1:]:
        total = total + ref[at].astype(F32)
    return total


def hidden_of(parts, *earlier):
    _, rows, width = parts[0].shape
    n = len(parts)

    def kernel(*refs):
        gate, up = total_of(refs[:n], 0), total_of(refs[:n], 1)
        refs[-2][...] = (jax.nn.silu(gate) * up).astype(BF16)

    return pl.pallas_call(
        kernel,
        in_specs=[whole_vmem()] * n + [token_spec()] * len(earlier),
        out_specs=[whole_vmem(), token_spec()],
        out_shape=[jax.ShapeDtypeStruct((rows, width), BF16), TOKEN],
        compiler_params=pltpu.CompilerParams(vmem_limit_bytes=SMALL),
        cost_estimate=LITTLE,
    )(*parts, *earlier)


def cotangents(chunks, grads, *earlier):
    n_c, rows, width = grads[0].shape
    n, n_g = len(chunks[0]), len(grads)

    def kernel(*refs):
        out_ref = refs[-1]
        for c in range(n_c):
            parts = refs[c * n:(c + 1) * n]
            grad = total_of(refs[n_c * n:n_c * n + n_g], c)
            gate, up = total_of(parts, 0), total_of(parts, 1)
            s = jax.nn.sigmoid(gate)
            out_ref[0, c] = (grad * up * s * (1.0 + gate * (1.0 - s))).astype(BF16)
            out_ref[1, c] = (grad * gate * s).astype(BF16)

    return pl.pallas_call(
        kernel,
        in_specs=[whole_vmem()] * (n_c * n + n_g) + [token_spec()] * len(earlier),
        out_specs=whole_vmem(),
        out_shape=jax.ShapeDtypeStruct((2, n_c, rows, width), BF16),
        compiler_params=pltpu.CompilerParams(vmem_limit_bytes=max(SMALL, 48 * n_c * rows * width)),
        cost_estimate=LITTLE,
    )(*[p for c in chunks for p in c], *grads, *earlier)


def weight_grads(panels, cots, masks, *earlier, cost=None):
    depth = panels[0].shape[1]
    width = cots[0][0].shape[1]
    tokens = sum(p.shape[0] for p in panels)
    block = depth // masks[0].shape[0]
    tile = tile_of(depth, 256)
    n_p, n_c, n_o = len(panels), len(cots[0]), len(cots)
    slots = 4

    def kernel(*refs):
        p_refs = refs[:n_p]
        c_refs = refs[n_p:n_p + n_c * n_o]
        m_refs = refs[n_p + n_c * n_o:n_p + n_c * n_o + n_o]
        out_refs = refs[-7 - n_o:-7]
        token_ref, cot, panel, out, kept, sem, fetch_sem = refs[-7:]
        low = 0
        fetches = [
            pltpu.make_async_copy(m_refs[o], kept.at[o], fetch_sem.at[n_p + o]) for o in range(n_o)
        ]
        for fetch in fetches:
            fetch.start()
        for index, ref in enumerate(p_refs):
            fetches.append(
                pltpu.make_async_copy(ref, panel.at[pl.ds(low, ref.shape[0])], fetch_sem.at[index])
            )
            fetches[-1].start()
            low += ref.shape[0]
        for o in range(n_o):
            low = 0
            for ref in c_refs[o * n_c:(o + 1) * n_c]:
                cot[o, low:low + ref.shape[0], :] = ref[...]
                low += ref.shape[0]
        for fetch in fetches:
            fetch.wait()
        copies = []
        for low in range(0, depth, tile):
            for o in range(n_o):
                slot = len(copies) % slots
                if len(copies) >= slots:
                    copies[-slots].wait()
                part = lax.dot_general(
                    panel[:, low:low + tile],
                    cot[o],
                    (((0,), (0,)), ((), ())),
                    preferred_element_type=F32,
                )
                out[slot] = masked(part, kept.at[o], low // block, block)
                copies.append(
                    pltpu.make_async_copy(
                        out.at[slot], out_refs[o].at[pl.ds(low, tile)], sem.at[slot]
                    )
                )
                copies[-1].start()
        for copy in copies[-slots:]:
            copy.wait()

    flat = [a for cot in cots for a in cot]
    out = jax.ShapeDtypeStruct((depth, width), F32)
    return pl.pallas_call(
        kernel,
        in_specs=[pl.BlockSpec(memory_space=pl.ANY)] * n_p
        + [whole_vmem()] * len(flat)
        + [pl.BlockSpec(memory_space=pl.ANY)] * n_o
        + [token_spec()] * len(earlier),
        out_specs=[pl.BlockSpec(memory_space=pl.ANY)] * n_o + [token_spec()],
        out_shape=[out] * n_o + [TOKEN],
        scratch_shapes=[
            pltpu.VMEM((n_o, tokens, width), BF16),
            pltpu.VMEM((tokens, depth), BF16),
            pltpu.VMEM((slots, tile, width), F32),
            pltpu.SMEM((n_o, *masks[0].shape), jnp.int32),
            pltpu.SemaphoreType.DMA((slots,)),
            pltpu.SemaphoreType.DMA((n_p + n_o,)),
        ],
        compiler_params=pltpu.CompilerParams(vmem_limit_bytes=LARGE),
        cost_estimate=cost
        or pl.CostEstimate(
            flops=2 * tokens * depth * width * n_o,
            bytes_accessed=4 * depth * width * n_o,
            transcendentals=0,
        ),
    )(*[hbm(p) for p in panels], *flat, *[hbm(m) for m in masks], *earlier)


def swap(value, axis, bits):
    size = lax.axis_size(axis)
    return lax.ppermute(value, axis, [(i, i ^ bits) for i in range(size)])


def exchange(pair):
    return [pair] + [swap(pair, "row", 2 * k) for k in range(1, lax.axis_size("row") // 2)]


def output_sum(parts, dtype, *earlier):
    n = len(parts)

    def kernel(*refs):
        refs[-2][...] = total_of(refs[:n], slice(None)).astype(dtype)

    return pl.pallas_call(
        kernel,
        in_specs=[whole_vmem()] * n + [token_spec()] * len(earlier),
        out_specs=[whole_vmem(), token_spec()],
        out_shape=[jax.ShapeDtypeStruct(parts[0].shape, dtype), TOKEN],
        compiler_params=pltpu.CompilerParams(vmem_limit_bytes=SMALL),
        cost_estimate=LITTLE,
    )(*parts, *earlier)


def per_device(tokens, out_grad, w_gate, w_up, w_down, mask_gate, mask_up, mask_down):
    rows = tokens.shape[0]
    n_k = lax.axis_size("col") // 2
    part = n_k // 2

    def places(chunk, k):
        return chunk, k // part, k % part

    evens = [tokens] + [swap(tokens, "col", 2 * k) for k in range(1, n_k)]
    own, swapped = join([tokens, swap(tokens, "col", 1)])
    panel, mine, theirs, token = panel_matmul(
        [(n_k - k if k else 0, 0, *places(0, k)) for k in range(n_k)],
        [own, *evens[:0:-1]],
        [w_gate, w_up],
        [mask_gate, mask_up],
        rows,
        swapped,
    )
    rest, _ = join(evens[1:], token)
    rest_odd = swap(rest, "col", 1)
    pair, first = add_blocks(mine, swap(theirs, "row", 1), 1)
    parts = exchange(pair)
    dz_even, joined = join([out_grad] + [swap(out_grad, "col", 2 * k) for k in range(1, n_k)], first)
    panel_odd, mine, theirs, token = panel_matmul(
        [(min(k, 1), max(k - 1, 0) * rows if k else rows, *places(0, k)) for k in range(n_k)],
        [own, rest_odd],
        [w_gate, w_up],
        [mask_gate, mask_up],
        rows,
        first,
        joined,
    )
    panels = [panel, panel_odd]
    step = (mine, swap(theirs, "row", 1))

    dz_arrays = [dz_even, swap(dz_even, "col", 1)]
    dz_pieces = [(c, k * rows, *places(c, k)) for c in range(2) for k in range(n_k)]

    chunks, hids, outs = [], [], []
    for c in range(2):
        chunks.append(parts)
        hid, formed = hidden_of(parts)
        pair, added = add_blocks(*step, 1, formed)
        parts = exchange(pair)
        other = swap(hid, "row", 1)
        *out, token = output_matmul(hid, other, w_down, mask_down, n_k)
        outs.append(out)
        hids += [hid, other]
        if c == 0:
            dz_panel, mine, theirs, token = panel_matmul(
                dz_pieces, dz_arrays, [w_down], [mask_down], rows, token
            )
            step = (mine, swap(theirs, "row", 1))
    own_share = outs[0][:1] + [swap(outs[0][k], "col", 2 * k) for k in range(1, n_k)]
    grad_down_w, token = weight_grads([dz_panel], [hids], [mask_down], token, cost=LITTLE)
    own_share, token = output_sum(own_share, F32, token)
    shares = [own_share] + [swap(outs[1][k], "col", 2 * k + 1) for k in range(n_k)]

    cot = cotangents(chunks, parts, token)
    other = swap(cot, "row", 1)
    cots = [[a[o, c] for c in range(2) for a in (cot, other)] for o in range(2)]
    grad_gate_w, grad_up_w, token = weight_grads(panels, cots, [mask_gate, mask_up])
    mixed, _ = output_sum(shares, BF16, token)
    return (mixed, grad_gate_w, grad_up_w, grad_down_w)


def solution(mesh):
    return jax.shard_map(
        per_device,
        mesh=mesh,
        in_specs=(P("col", "row"),) * 2 + (P("row", "col"),) * 6,
        out_specs=(P("col", "row"),) + (P("row", "col"),) * 3,
        check_vma=False,
    )
```
